32 devices in a mesh: seq: 8 (over y, x, core), db: 4 (over z).
Axes of the slice: x: 2, y: 2, z: 4, core: 2. Of those that a mesh axis runs over, the one named last changes fastest.
Arguments:
- decoder: bfloat16 [8192, 4096], P('seq'), may hold values from -6 to 6
- w_query: bfloat16 [4096, 4096], P(None, 'db'), may hold values from -0.09375 to 0.09375
- w_key: bfloat16 [896, 4096], P(None, 'db'), may hold values from -0.1875 to 0.1875
- w_value: bfloat16 [896, 4096], P(None, 'db'), may hold values from -0.1875 to 0.1875
- w_out: bfloat16 [4096, 4096], P('db'), may hold values from -0.09375 to 0.09375
- database: bfloat16 [192, 128, 896], P('seq'), may hold values from -240 to 240
- nb_shard: int32 [128, 2], replicated, may hold values from 0 to 7, as said below
- nb_slot: int32 [128, 2], replicated, may hold values from 0 to 23
Outputs:
- attended: bfloat16 [8192, 4096], P(('seq', 'db'))
The draws below stay inside these ranges and needn't reach their ends.
Inputs may be any that keep to these rules, and one draw needn't show every extreme that they name: `nb_shard`: the 32 entries of each 16 consecutive spans name any one shard at most 5 times, and one shard exactly 5 times.
All inputs are finite; a program needn't handle non-finite values.
Results may differ from the reference program's by a relative error of at most 0.022.
The reference program's roundings to bfloat16 on the way (of `normed`, `queries`, `keys`, `values`, `probs` and `context`) count: a program that leaves them out, or rounds other values in their place, can miss the bound.
Values may be sent and summed in bfloat16 or wider, within the bound.
A program may use at most 128 MiB of HBM per device.

```python
import math
import jax
import jax.numpy as jnp
from jax import lax

D = 4096
HEADS = 32
HS = 128
EW = 896
CL = 64
NB_LEN = 128
NEIGH = 2
CH_SEQ = 16
SLOTS = 24
TOKENS = 8192
SPANS = 128
SHARDS = 8
NREQ = 32
CAP = 5
N_SEQ = 8
N_DB = 4


def draw_nb_shard(key, part):
    key = jax.random.fold_in(key, 7)

    def one_group(group_key):
        key_hot, key_rest, key_order = jax.random.split(group_key, 3)
        hottest = jax.random.randint(key_hot, (), 0, SHARDS).astype(jnp.int32)
        places = jax.random.permutation(key_rest, (SHARDS - 1) * CAP)[:NREQ - CAP]
        others = (places // CAP).astype(jnp.int32)
        others = others + (others >= hottest).astype(jnp.int32)
        listed = jnp.concatenate([jnp.full((CAP,), hottest, jnp.int32), others])
        return jax.random.permutation(key_order, listed)
    groups = jax.vmap(one_group)(jax.random.split(key, SHARDS))
    return groups.reshape(SPANS, NEIGH).astype(jnp.int32)


def draw_database(key, part):
    key = jax.random.fold_in(key, 19)
    key_base = jax.random.fold_in(key, 0)
    base = jnp.clip(jax.random.normal(key_base, (SHARDS * SLOTS, NB_LEN, EW), jnp.float32), -6.0, 6.0)
    return base.astype(jnp.bfloat16)


def plant(array, stream_key, smallest, top_value):
    longest = array.shape.index(max(array.shape))
    spots = []
    for shift in (0, 1):
        where = [jax.random.randint(jax.random.fold_in(stream_key, axis), (), 0, length) for axis, length in enumerate(array.shape)]
        where[longest] = (where[longest] + shift) % array.shape[longest]
        spots.append(tuple(where))
    return array.at[spots[0]].set(smallest).at[spots[1]].set(top_value)


def steps_of(own_key, shape, cuts, smallest, high):
    def one(axis_at, blocks):
        steps = jax.random.uniform(jax.random.fold_in(jax.random.fold_in(own_key, 6), axis_at), (blocks,), jnp.float32, smallest / len(cuts), high / len(cuts))
        return jnp.repeat(jnp.exp(steps), shape[axis_at] // blocks).reshape((-1,) + (1,) * (len(shape) - axis_at - 1))

    level = one(*cuts[0])
    for cut in cuts[1:]:
        level = level * one(*cut)
    return level


def bell_draw(key, extent, scale, bound, cuts=(), held_as=jnp.bfloat16):
    gain = steps_of(key, extent, cuts, -0.22, 0.18) if cuts else 1.0
    array = jax.random.normal(key, extent, jnp.float32) * scale * gain
    return jnp.minimum(jnp.maximum(array, -bound), bound).astype(held_as)


def setup_inputs(seed: int = 0) -> dict:
    key_of = jax.random.split(jax.random.key(seed), 9)
    decoder = bell_draw(key_of[0], (TOKENS, D), 1.0, 6.0, ((0, 8),))
    w_query = bell_draw(key_of[1], (D, HEADS * HS), D ** -0.5, 0.09375, ((1, 4),))
    w_key = bell_draw(key_of[2], (EW, HEADS * HS), EW ** -0.5, 0.1875, ((1, 4),))
    w_value = bell_draw(key_of[3], (EW, HEADS * HS), EW ** -0.5, 0.1875, ((1, 4),))
    w_out = bell_draw(key_of[4], (HEADS * HS, D), (HEADS * HS) ** -0.5, 0.09375, ((0, 4),))
    database = draw_database(jax.random.fold_in(key_of[8], 71), 0)
    nb_shard = draw_nb_shard(jax.random.fold_in(key_of[8], 71), 0)
    nb_slot = plant(jax.random.randint(key_of[7], (SPANS, NEIGH), 0, SLOTS), jax.random.fold_in(key_of[7], 1), 0, SLOTS - 1).astype(jnp.int32)
    return dict(decoder=decoder, w_query=w_query, w_key=w_key, w_value=w_value, w_out=w_out, database=database, nb_shard=nb_shard, nb_slot=nb_slot)


def attend(queries, keys, values):
    blocks, qlen, width = queries.shape
    heads_here = width // HS
    q_heads = queries.astype(jnp.float32).reshape(blocks, qlen, heads_here, HS)
    k_heads = keys.astype(jnp.float32).reshape(blocks, keys.shape[1], heads_here, HS)
    v_heads = values.astype(jnp.float32).reshape(blocks, values.shape[1], heads_here, HS)
    scores = jnp.einsum('bqhd,bkhd->bhqk', q_heads, k_heads) * (1.0 / math.sqrt(HS))
    probs = jax.nn.softmax(scores, axis=-1).astype(jnp.bfloat16)
    context = jnp.einsum('bhqk,bkhd->bqhd', probs.astype(jnp.float32), v_heads)
    return context.reshape(blocks, qlen, width).astype(jnp.bfloat16)

def reference(decoder, w_query, w_key, w_value, w_out, database, nb_shard, nb_slot):
    source = decoder.astype(jnp.float32)
    scale = lax.rsqrt(lax.optimization_barrier(jnp.mean(source * source, axis=-1, keepdims=True)) + 1e-05)
    normed = (source * scale).astype(jnp.bfloat16)
    queries = jnp.dot(normed, w_query, preferred_element_type=jnp.float32).astype(jnp.bfloat16)
    width = queries.shape[1]
    shifted = jnp.concatenate([queries[CL - 1:], jnp.zeros((CL - 1, width), jnp.bfloat16)], axis=0)
    shifted = shifted.reshape(N_SEQ, CH_SEQ, CL, width)
    flat_index = (nb_shard * SLOTS + nb_slot).astype(jnp.int32).reshape(N_SEQ, CH_SEQ * NEIGH)
    key_weight = w_key.astype(jnp.float32)
    value_weight = w_value.astype(jnp.float32)

    def one_block(inputs):
        block_queries, block_index = inputs
        rows = database[block_index].reshape(CH_SEQ, NEIGH * NB_LEN, EW).astype(jnp.float32)
        keys = jnp.einsum('cne,eh->cnh', rows, key_weight).astype(jnp.bfloat16)
        values = jnp.einsum('cne,eh->cnh', rows, value_weight).astype(jnp.bfloat16)
        return attend(block_queries, keys, values)
    aligned = lax.map(one_block, (shifted, flat_index)).reshape(TOKENS, width)
    context = jnp.concatenate([jnp.zeros((CL - 1, width), jnp.bfloat16), aligned[:TOKENS - CL + 1]], axis=0)
    group_width = width // N_DB
    total = jnp.zeros((TOKENS, D), jnp.float32)
    for head_group in range(N_DB):
        lower = head_group * group_width
        partial_sum = jnp.dot(context[:, lower:lower + group_width], w_out[lower:lower + group_width], preferred_element_type=jnp.float32).astype(jnp.bfloat16)
        total = total + lax.optimization_barrier(partial_sum).astype(jnp.float32)
    return total.astype(jnp.bfloat16)
```

```python
import functools
import math

import jax
import jax.numpy as jnp
from jax import lax
from jax.experimental import pallas as pl
from jax.experimental.pallas import tpu as pltpu
from jax.sharding import PartitionSpec as P

HS = 128
CL = 64
NB_LEN = 128
NEIGH = 2


def shifted(value, axis, steps):
    count = lax.axis_size(axis)
    first, last = (max(0, -steps), min(count, count - steps))
    return lax.ppermute(value, axis, [(source, source + steps) for source in range(first, last)])


def bucket_places(shards):
    count = shards.shape[1]
    same_shard = shards[:, :, None] == shards[:, None, :]
    earlier = jnp.arange(count)[None, :] < jnp.arange(count)[:, None]
    return jnp.sum((same_shard & earlier[None]).astype(jnp.int32), axis=2)


def attend_kernel(spans, first, second, q_ref, rows0, rows1, wk_ref, wv_ref, o_ref):
    rows = jnp.concatenate([rows0[0], rows1[0]], axis=0)
    keys = jnp.dot(rows, wk_ref[...], preferred_element_type=jnp.float32).astype(jnp.bfloat16)
    values = jnp.dot(rows, wv_ref[...], preferred_element_type=jnp.float32).astype(jnp.bfloat16)
    queries = q_ref[0]
    for head in range(queries.shape[1] // HS):
        cut = slice(head * HS, (head + 1) * HS)
        scores = lax.dot_general(
            queries[:, cut],
            keys[:, cut],
            (((1,), (1,)), ((), ())),
            preferred_element_type=jnp.float32,
        ) * (1.0 / math.sqrt(HS))
        weights = jnp.exp(scores - jnp.max(scores, axis=-1, keepdims=True))
        probs = (weights / jnp.sum(weights, axis=-1, keepdims=True)).astype(jnp.bfloat16)
        o_ref[0, :, cut] = jnp.dot(
            probs, values[:, cut], preferred_element_type=jnp.float32
        ).astype(jnp.bfloat16)


def attend(spans, entries, queries, rows, w_key, w_value):
    count = spans.shape[0]
    _, qlen, width = queries.shape
    _, nb_len, depth = rows.shape
    grid_spec = pltpu.PrefetchScalarGridSpec(
        num_scalar_prefetch=3,
        grid=(count,),
        in_specs=[
            pl.BlockSpec((1, qlen, width), lambda g, s, a, b: (s[g], 0, 0)),
            pl.BlockSpec((1, nb_len, depth), lambda g, s, a, b: (a[g], 0, 0)),
            pl.BlockSpec((1, nb_len, depth), lambda g, s, a, b: (b[g], 0, 0)),
            pl.BlockSpec((depth, width), lambda g, s, a, b: (0, 0)),
            pl.BlockSpec((depth, width), lambda g, s, a, b: (0, 0)),
        ],
        out_specs=pl.BlockSpec((1, qlen, width), lambda g, s, a, b: (g, 0, 0)),
    )
    keys_len = NEIGH * nb_len
    return pl.pallas_call(
        attend_kernel,
        grid_spec=grid_spec,
        out_shape=jax.ShapeDtypeStruct((count, qlen, width), jnp.bfloat16),
        compiler_params=pltpu.CompilerParams(vmem_limit_bytes=40 * 1024 * 1024),
        cost_estimate=pl.CostEstimate(
            flops=count * (4 * keys_len * depth * width + 4 * qlen * keys_len * width),
            bytes_accessed=count * 2 * (keys_len * depth + 2 * qlen * width) + 4 * depth * width,
            transcendentals=count * qlen * keys_len * width // HS,
        ),
        name="attend",
    )(spans, entries[spans, 0], entries[spans, 1], queries, rows, rows, w_key, w_value)


def body(decoder, w_query, w_key, w_value, w_out, database, nb_shard, nb_slot):
    n_seq = lax.axis_size("seq")
    n_db = lax.axis_size("db")
    seq_index = lax.axis_index("seq")
    db_index = lax.axis_index("db")
    tok_rows = decoder.shape[0]
    spans_dev = tok_rows // CL
    width = w_query.shape[1]
    requests = NEIGH * spans_dev
    capacity = (requests + n_seq - 1) // n_seq + 1
    shard_lists = nb_shard.reshape(n_seq, requests)
    slot_lists = nb_slot.reshape(n_seq, requests)
    places = bucket_places(shard_lists)
    mine = shard_lists == seq_index
    picked = mine[:, None, :] & (places[:, None, :] == jnp.arange(capacity)[None, :, None])
    send_slot = jnp.sum(jnp.where(picked, slot_lists[:, None, :], 0), axis=2)
    outgoing = database[send_slot]
    received = lax.all_to_all(outgoing, "seq", split_axis=0, concat_axis=0, tiled=True)
    my_shards = lax.dynamic_index_in_dim(shard_lists, seq_index, 0, keepdims=False)
    my_places = lax.dynamic_index_in_dim(places, seq_index, 0, keepdims=False)
    entries = (my_shards * capacity + my_places).reshape(spans_dev, NEIGH)
    rows = received.reshape(n_seq * capacity, NB_LEN, received.shape[3])
    swap = [(source, source ^ 1) for source in range(n_db)]
    part = w_out.shape[0] // n_seq
    w_part = lax.dynamic_slice_in_dim(w_out, seq_index * part, part, 0)
    w_other = lax.all_gather(lax.ppermute(w_part, "db", swap), "seq", axis=0, tiled=True)
    source = decoder.astype(jnp.float32)
    scale = lax.rsqrt(jnp.mean(source * source, axis=-1, keepdims=True) + 1e-05)
    normed = (source * scale).astype(jnp.bfloat16)
    queries = jnp.dot(normed, w_query, preferred_element_type=jnp.float32).astype(jnp.bfloat16)
    incoming = shifted(queries[: CL - 1], "seq", -1)
    aligned_queries = jnp.concatenate([queries[CL - 1 :], incoming], axis=0).reshape(
        spans_dev, CL, width
    )
    blocks = n_db // 2
    block_spans = spans_dev // n_db
    chunks = 2 if block_spans % 2 == 0 else 1
    chunk_spans = block_spans // chunks
    steps = 2 * jnp.arange(blocks)

    def spans_of(owner, chunk):
        block = lax.rem(owner + steps, n_db)
        inner = chunk * chunk_spans + jnp.arange(chunk_spans)
        return (block[:, None] * block_spans + inner[None, :]).reshape(-1).astype(jnp.int32)

    done = [None] * chunks
    for chunk in reversed(range(chunks)):
        theirs = attend(
            spans_of(db_index ^ 1, chunk), entries, aligned_queries, rows, w_key, w_value
        )
        from_pair = lax.ppermute(theirs, "db", swap)
        ours = attend(spans_of(db_index, chunk), entries, aligned_queries, rows, w_key, w_value)
        size = chunk_spans * CL
        total = jnp.dot(
            ours.reshape(-1, width), w_out, preferred_element_type=jnp.float32
        ) + jnp.dot(from_pair.reshape(-1, width), w_other, preferred_element_type=jnp.float32)
        partial = total.astype(jnp.bfloat16).reshape(blocks, size, -1)
        result = partial[0].astype(jnp.float32)
        for step in range(1, blocks):
            pairs = [(source, (source + 2 * step) % n_db) for source in range(n_db)]
            result = result + lax.ppermute(partial[step], "db", pairs).astype(jnp.float32)
        done[chunk] = result.astype(jnp.bfloat16)
    flat = n_seq * n_db
    halo = lax.ppermute(
        done[-1][-(CL - 1) :], ("seq", "db"), [(source, source + 1) for source in range(flat - 1)]
    )
    return jnp.concatenate([halo] + done[:-1] + [done[-1][: -(CL - 1)]], axis=0)


def solution(mesh):
    return jax.shard_map(
        body,
        mesh=mesh,
        in_specs=(
            P("seq", None),
            P(None, "db"),
            P(None, "db"),
            P(None, "db"),
            P("db", None),
            P("seq", None, None),
            P(),
            P(),
        ),
        out_specs=P(("seq", "db"), None),
        check_vma=False,
    )
```

```python
import functools
import math

import jax
import jax.numpy as jnp
from jax import lax
from jax.experimental import pallas as pl
from jax.experimental.pallas import tpu as pltpu
from jax.sharding import PartitionSpec as P

HS = 128
CL = 64
NB_LEN = 128
NEIGH = 2


def shifted(value, axis, steps):
    count = lax.axis_size(axis)
    first, last = (max(0, -steps), min(count, count - steps))
    return lax.ppermute(value, axis, [(source, source + steps) for source in range(first, last)])


def bucket_places(shards):
    count = shards.shape[1]
    same_shard = shards[:, :, None] == shards[:, None, :]
    earlier = jnp.arange(count)[None, :] < jnp.arange(count)[:, None]
    return jnp.sum((same_shard & earlier[None]).astype(jnp.int32), axis=2)


def attend_kernel(spans, first, second, *refs):
    per_step = (len(refs) - 3) // 3
    q_refs, row_refs = refs[:per_step], refs[per_step : 3 * per_step]
    wk_ref, wv_ref, o_ref = refs[3 * per_step :]
    rows = jnp.concatenate([ref[0] for ref in row_refs], axis=0)
    keys = jnp.dot(rows, wk_ref[...], preferred_element_type=jnp.float32).astype(jnp.bfloat16)
    values = jnp.dot(rows, wv_ref[...], preferred_element_type=jnp.float32).astype(jnp.bfloat16)
    keys_len = keys.shape[0] // per_step
    for place in range(per_step):
        here = slice(place * keys_len, (place + 1) * keys_len)
        for head in range(keys.shape[1] // HS):
            cut = slice(head * HS, (head + 1) * HS)
            scores = lax.dot_general(
                q_refs[place][0, :, cut],
                keys[here, cut],
                (((1,), (1,)), ((), ())),
                preferred_element_type=jnp.float32,
            )
            top = jnp.max(scores, axis=-1, keepdims=True)
            weights = jnp.exp((scores - top) * (1.0 / math.sqrt(HS)))
            probs = weights * (1.0 / jnp.sum(weights, axis=-1, keepdims=True))
            o_ref[place, :, cut] = jnp.dot(
                probs.astype(jnp.bfloat16), values[here, cut], preferred_element_type=jnp.float32
            ).astype(jnp.bfloat16)


def attend(spans, entries, queries, rows, w_key, w_value):
    count = spans.shape[0]
    per_step = 2 if count % 2 == 0 else 1
    _, qlen, width = queries.shape
    _, nb_len, depth = rows.shape
    q_specs, row_specs = [], []
    for place in range(per_step):
        q_specs.append(
            pl.BlockSpec(
                (1, qlen, width), lambda g, s, a, b, place=place: (s[g * per_step + place], 0, 0)
            )
        )
        row_specs.append(
            pl.BlockSpec(
                (1, nb_len, depth), lambda g, s, a, b, place=place: (a[g * per_step + place], 0, 0)
            )
        )
        row_specs.append(
            pl.BlockSpec(
                (1, nb_len, depth), lambda g, s, a, b, place=place: (b[g * per_step + place], 0, 0)
            )
        )
    whole = pl.BlockSpec((depth, width), lambda g, s, a, b: (0, 0))
    grid_spec = pltpu.PrefetchScalarGridSpec(
        num_scalar_prefetch=3,
        grid=(count // per_step,),
        in_specs=q_specs + row_specs + [whole, whole],
        out_specs=pl.BlockSpec((per_step, qlen, width), lambda g, s, a, b: (g, 0, 0)),
    )
    keys_len = NEIGH * nb_len
    operands = [queries] * per_step + [rows] * (NEIGH * per_step) + [w_key, w_value]
    return pl.pallas_call(
        attend_kernel,
        grid_spec=grid_spec,
        out_shape=jax.ShapeDtypeStruct((count, qlen, width), jnp.bfloat16),
        compiler_params=pltpu.CompilerParams(vmem_limit_bytes=44 * 1024 * 1024),
        cost_estimate=pl.CostEstimate(
            flops=count * (4 * keys_len * depth * width + 4 * qlen * keys_len * width),
            bytes_accessed=count * 2 * (keys_len * depth + 2 * qlen * width) + 4 * depth * width,
            transcendentals=count * qlen * keys_len * width // HS,
        ),
        name="attend",
    )(spans, entries[spans, 0], entries[spans, 1], *operands)


def project_kernel(x_ref, y_ref, z_ref, wx_ref, wy_ref, wz_ref, rest_ref, last_ref):
    total = jnp.dot(x_ref[...], wx_ref[...], preferred_element_type=jnp.float32)
    total += jnp.dot(y_ref[...], wy_ref[...], preferred_element_type=jnp.float32)
    total += jnp.dot(z_ref[...], wz_ref[...], preferred_element_type=jnp.float32)
    total = total.astype(jnp.bfloat16)
    cut = rest_ref.shape[0]
    rest_ref[...] = total[:cut]
    last_ref[...] = total[cut:]


def project(x, y, z, w_x, w_y, w_z):
    size, width = x.shape
    features = w_x.shape[1]
    tile = 512
    own = lambda array: pl.BlockSpec(array.shape, lambda g: (0, 0))
    strip = lambda array: pl.BlockSpec((array.shape[0], tile), lambda g: (0, g))
    return pl.pallas_call(
        project_kernel,
        grid=(features // tile,),
        in_specs=[own(x), own(y), own(z), strip(w_x), strip(w_y), strip(w_z)],
        out_specs=[
            pl.BlockSpec((size - CL, tile), lambda g: (0, g)),
            pl.BlockSpec((CL, tile), lambda g: (0, g)),
        ],
        out_shape=[
            jax.ShapeDtypeStruct((size - CL, features), jnp.bfloat16),
            jax.ShapeDtypeStruct((CL, features), jnp.bfloat16),
        ],
        compiler_params=pltpu.CompilerParams(vmem_limit_bytes=40 * 1024 * 1024),
        cost_estimate=pl.CostEstimate(
            flops=4 * size * width * features,
            bytes_accessed=4 * width * features + 2 * size * features,
            transcendentals=0,
        ),
        name="project",
    )(x, y, z, w_x, w_y, w_z)


def body(decoder, w_query, w_key, w_value, w_out, database, nb_shard, nb_slot):
    n_seq = lax.axis_size("seq")
    n_db = lax.axis_size("db")
    seq_index = lax.axis_index("seq")
    db_index = lax.axis_index("db")
    tok_rows = decoder.shape[0]
    spans_dev = tok_rows // CL
    width = w_query.shape[1]
    requests = NEIGH * spans_dev
    capacity = (requests + n_seq - 1) // n_seq + 1
    shard_lists = nb_shard.reshape(n_seq, requests)
    slot_lists = nb_slot.reshape(n_seq, requests)
    places = bucket_places(shard_lists)
    mine = shard_lists == seq_index
    picked = mine[:, None, :] & (places[:, None, :] == jnp.arange(capacity)[None, :, None])
    send_slot = jnp.sum(jnp.where(picked, slot_lists[:, None, :], 0), axis=2)
    outgoing = database[send_slot]
    received = lax.all_to_all(outgoing, "seq", split_axis=0, concat_axis=0, tiled=True)
    my_shards = lax.dynamic_index_in_dim(shard_lists, seq_index, 0, keepdims=False)
    my_places = lax.dynamic_index_in_dim(places, seq_index, 0, keepdims=False)
    entries = (my_shards * capacity + my_places).reshape(spans_dev, NEIGH)
    rows = received.reshape(n_seq * capacity, NB_LEN, received.shape[3])
    swap = [(source, source ^ 1) for source in range(n_db)]
    half = w_out.shape[0] // 2
    my_half = lax.rem(seq_index, 2)
    w_near = lax.ppermute(
        lax.dynamic_slice_in_dim(w_out, my_half * half, half, 0), "db", swap
    )
    w_near, rows = lax.optimization_barrier((w_near, rows))
    w_far = lax.ppermute(w_near, "seq", [(source, source ^ 1) for source in range(n_seq)])
    source = decoder.astype(jnp.float32)
    scale = lax.rsqrt(jnp.mean(source * source, axis=-1, keepdims=True) + 1e-05)
    normed = (source * scale).astype(jnp.bfloat16)
    queries = jnp.dot(normed, w_query, preferred_element_type=jnp.float32).astype(jnp.bfloat16)
    incoming = shifted(queries[: CL - 1], "seq", -1)
    aligned_queries = jnp.concatenate([queries[CL - 1 :], incoming], axis=0).reshape(
        spans_dev, CL, width
    )
    blocks = n_db // 2
    block_spans = spans_dev // n_db

    def spans_of(owner, step):
        block = lax.rem(owner + 2 * step, n_db)
        return (block * block_spans + jnp.arange(block_spans)).astype(jnp.int32)

    def partial_of(step, queries):
        theirs = attend(spans_of(db_index ^ 1, step), entries, queries, rows, w_key, w_value)
        from_pair = lax.ppermute(theirs, "db", swap).reshape(-1, width)
        ours = attend(spans_of(db_index, step), entries, queries, rows, w_key, w_value)
        near = lax.dynamic_slice_in_dim(from_pair, my_half * half, half, 1)
        far = lax.dynamic_slice_in_dim(from_pair, (1 - my_half) * half, half, 1)
        return project(ours.reshape(-1, width), near, far, w_out, w_near, w_far)

    rests, lasts = [], []
    for step in range(1, blocks):
        rest, last = partial_of(step, aligned_queries)
        rest, last, aligned_queries = lax.optimization_barrier((rest, last, aligned_queries))
        pairs = [(source, (source + 2 * step) % n_db) for source in range(n_db)]
        lasts.append(lax.ppermute(last, "db", pairs))
        rests.append(lax.ppermute(rest, "db", pairs))
    rest, last = partial_of(0, aligned_queries)
    last = sum([value.astype(jnp.float32) for value in lasts], last.astype(jnp.float32))
    last = last.astype(jnp.bfloat16)
    flat = n_seq * n_db
    halo = lax.ppermute(
        last[1:], ("seq", "db"), [(source, source + 1) for source in range(flat - 1)]
    )
    rest = sum([value.astype(jnp.float32) for value in rests], rest.astype(jnp.float32))
    return jnp.concatenate([halo, rest.astype(jnp.bfloat16), last[:1]], axis=0)


def solution(mesh):
    return jax.shard_map(
        body,
        mesh=mesh,
        in_specs=(
            P("seq", None),
            P(None, "db"),
            P(None, "db"),
            P(None, "db"),
            P("db", None),
            P("seq", None, None),
            P(),
            P(),
        ),
        out_specs=P(("seq", "db"), None),
        check_vma=False,
    )
```

```python
import functools
import math

import jax
import jax.numpy as jnp
from jax import lax
from jax.experimental import pallas as pl
from jax.experimental.pallas import tpu as pltpu
from jax.sharding import PartitionSpec as P

HS = 128
CL = 64
NB_LEN = 128
NEIGH = 2


def shifted(value, axis, steps):
    count = lax.axis_size(axis)
    first, last = (max(0, -steps), min(count, count - steps))
    return lax.ppermute(value, axis, [(source, source + steps) for source in range(first, last)])


def bucket_places(shards):
    count = shards.shape[1]
    same_shard = shards[:, :, None] == shards[:, None, :]
    earlier = jnp.arange(count)[None, :] < jnp.arange(count)[:, None]
    return jnp.sum((same_shard & earlier[None]).astype(jnp.int32), axis=2)


def attend_kernel(first, entries, *refs):
    per_step = (len(refs) - 3) // 3
    q_refs, row_refs = refs[:per_step], refs[per_step : 3 * per_step]
    wk_ref, wv_ref, o_ref = refs[3 * per_step :]
    rows = jnp.concatenate([ref[0] for ref in row_refs], axis=0)
    keys = jnp.dot(rows, wk_ref[...], preferred_element_type=jnp.float32).astype(jnp.bfloat16)
    keys_len, qlen = keys.shape[0] // per_step, q_refs[0].shape[1]
    units = [
        (place, slice(place * keys_len, (place + 1) * keys_len), slice(at, at + HS))
        for place in range(per_step)
        for at in range(0, keys.shape[1], HS)
    ]
    scores = jnp.concatenate(
        [
            lax.dot_general(
                q_refs[place][0, :, cut],
                keys[here, cut],
                (((1,), (1,)), ((), ())),
                preferred_element_type=jnp.float32,
            )
            for place, here, cut in units
        ],
        axis=0,
    )
    values = jnp.dot(rows, wv_ref[...], preferred_element_type=jnp.float32).astype(jnp.bfloat16)
    top = jnp.max(scores, axis=-1, keepdims=True)
    weights = jnp.exp((scores - top) * (1.0 / math.sqrt(HS)))
    probs = weights * (1.0 / jnp.sum(weights, axis=-1, keepdims=True))
    probs = probs.astype(jnp.bfloat16)
    for at, (place, here, cut) in enumerate(units):
        o_ref[place, :, cut] = jnp.dot(
            probs[at * qlen : (at + 1) * qlen],
            values[here, cut],
            preferred_element_type=jnp.float32,
        ).astype(jnp.bfloat16)


def attend(first, count, entries, queries, rows, w_key, w_value):
    per_step = 2 if count % 2 == 0 else 1
    _, qlen, width = queries.shape
    _, nb_len, depth = rows.shape

    def query_block(place):
        return pl.BlockSpec(
            (1, qlen, width), lambda g, f, e: (f[0] + g * per_step + place, 0, 0)
        )

    def row_block(place, which):
        return pl.BlockSpec(
            (1, nb_len, depth),
            lambda g, f, e: (e[(f[0] + g * per_step + place) * NEIGH + which], 0, 0),
        )

    whole = pl.BlockSpec((depth, width), lambda g, f, e: (0, 0))
    grid_spec = pltpu.PrefetchScalarGridSpec(
        num_scalar_prefetch=2,
        grid=(count // per_step,),
        in_specs=[query_block(place) for place in range(per_step)]
        + [row_block(place, which) for place in range(per_step) for which in range(NEIGH)]
        + [whole, whole],
        out_specs=pl.BlockSpec((per_step, qlen, width), lambda g, f, e: (g, 0, 0)),
    )
    operands = [queries] * per_step + [rows] * (NEIGH * per_step) + [w_key, w_value]
    return pl.pallas_call(
        attend_kernel,
        grid_spec=grid_spec,
        out_shape=jax.ShapeDtypeStruct((count, qlen, width), jnp.bfloat16),
        compiler_params=pltpu.CompilerParams(vmem_limit_bytes=56 * 1024 * 1024),
        cost_estimate=pl.CostEstimate(flops=1000, bytes_accessed=1000, transcendentals=0),
        name="attend",
    )(first.reshape(1).astype(jnp.int32), entries, *operands)


def project_kernel(x_ref, y_ref, z_ref, wx_ref, wy_ref, wz_ref, rest_ref, last_ref):
    total = jnp.dot(x_ref[...], wx_ref[...], preferred_element_type=jnp.float32)
    total += jnp.dot(y_ref[...], wy_ref[...], preferred_element_type=jnp.float32)
    total += jnp.dot(z_ref[...], wz_ref[...], preferred_element_type=jnp.float32)
    total = total.astype(jnp.bfloat16)
    cut = rest_ref.shape[0]
    rest_ref[...] = total[:cut]
    last_ref[...] = total[cut:]


def project(x, y, z, w_x, w_y, w_z):
    size, width = x.shape
    features = w_x.shape[1]
    tile = 512
    own = lambda array: pl.BlockSpec(array.shape, lambda g: (0, 0))
    strip = lambda array: pl.BlockSpec((array.shape[0], tile), lambda g: (0, g))
    return pl.pallas_call(
        project_kernel,
        grid=(features // tile,),
        in_specs=[own(x), own(y), own(z), strip(w_x), strip(w_y), strip(w_z)],
        out_specs=[
            pl.BlockSpec((size - CL, tile), lambda g: (0, g)),
            pl.BlockSpec((CL, tile), lambda g: (0, g)),
        ],
        out_shape=[
            jax.ShapeDtypeStruct((size - CL, features), jnp.bfloat16),
            jax.ShapeDtypeStruct((CL, features), jnp.bfloat16),
        ],
        compiler_params=pltpu.CompilerParams(vmem_limit_bytes=40 * 1024 * 1024),
        cost_estimate=pl.CostEstimate(flops=1000, bytes_accessed=1000, transcendentals=0),
        name="project",
    )(x, y, z, w_x, w_y, w_z)


def body(decoder, w_query, w_key, w_value, w_out, database, nb_shard, nb_slot):
    n_seq = lax.axis_size("seq")
    n_db = lax.axis_size("db")
    seq_index = lax.axis_index("seq")
    db_index = lax.axis_index("db")
    tok_rows = decoder.shape[0]
    spans_dev = tok_rows // CL
    width = w_query.shape[1]
    requests = NEIGH * spans_dev
    capacity = (requests + n_seq - 1) // n_seq + 1
    shard_lists = nb_shard.reshape(n_seq, requests)
    slot_lists = nb_slot.reshape(n_seq, requests)
    places = bucket_places(shard_lists)
    mine = shard_lists == seq_index
    picked = mine[:, None, :] & (places[:, None, :] == jnp.arange(capacity)[None, :, None])
    send_slot = jnp.sum(jnp.where(picked, slot_lists[:, None, :], 0), axis=2)
    outgoing = database[send_slot]
    received = lax.all_to_all(outgoing, "seq", split_axis=0, concat_axis=0, tiled=True)
    my_shards = lax.dynamic_index_in_dim(shard_lists, seq_index, 0, keepdims=False)
    my_places = lax.dynamic_index_in_dim(places, seq_index, 0, keepdims=False)
    entries = my_shards * capacity + my_places
    rows = received.reshape(n_seq * capacity, NB_LEN, received.shape[3])
    swap = [(source, source ^ 1) for source in range(n_db)]
    half = w_out.shape[0] // 2
    my_half = lax.rem(seq_index, 2)
    w_near = lax.ppermute(
        lax.dynamic_slice_in_dim(w_out, my_half * half, half, 0), "db", swap
    )
    source = decoder.astype(jnp.float32)
    scale = lax.rsqrt(jnp.mean(source * source, axis=-1, keepdims=True) + 1e-05)
    normed = (source * scale).astype(jnp.bfloat16)
    queries = jnp.dot(normed, w_query, preferred_element_type=jnp.float32).astype(jnp.bfloat16)
    incoming = shifted(queries[: CL - 1], "seq", -1)
    aligned_queries = jnp.concatenate([queries[CL - 1 :], incoming], axis=0).reshape(
        spans_dev, CL, width
    )
    w_near, rows, aligned_queries = lax.optimization_barrier((w_near, rows, aligned_queries))
    near_seq = [(source, source ^ 1) for source in range(n_seq)]
    w_far = lax.ppermute(w_near, "seq", near_seq)
    blocks = n_db // 2
    block_spans = spans_dev // n_db

    def attend_block(owner, step, queries):
        first = lax.rem(owner + 2 * step, n_db) * block_spans
        return attend(first, block_spans, entries, queries, rows, w_key, w_value)

    def partial_of(step, queries):
        theirs = attend_block(db_index ^ 1, step, queries)
        from_pair = lax.ppermute(theirs, "db", swap).reshape(-1, width)
        ours = attend_block(db_index, step, queries)
        near = lax.dynamic_slice_in_dim(from_pair, my_half * half, half, 1)
        far = lax.dynamic_slice_in_dim(from_pair, (1 - my_half) * half, half, 1)
        return project(ours.reshape(-1, width), near, far, w_out, w_near, w_far)

    rests, lasts = [], []
    for step in range(1, blocks):
        rest, last = partial_of(step, aligned_queries)
        pairs = [(source, (source + 2 * step) % n_db) for source in range(n_db)]
        lasts.append(lax.ppermute(last, "db", pairs))
        rests.append(lax.ppermute(rest, "db", pairs))
    rest, last = partial_of(0, aligned_queries)
    last = sum([value.astype(jnp.float32) for value in lasts], last.astype(jnp.float32))
    last = last.astype(jnp.bfloat16)
    flat = n_seq * n_db
    halo = lax.ppermute(
        last[1:], ("seq", "db"), [(source, source + 1) for source in range(flat - 1)]
    )
    rest = sum([value.astype(jnp.float32) for value in rests], rest.astype(jnp.float32))
    return jnp.concatenate([halo, rest.astype(jnp.bfloat16), last[:1]], axis=0)


def solution(mesh):
    return jax.shard_map(
        body,
        mesh=mesh,
        in_specs=(
            P("seq", None),
            P(None, "db"),
            P(None, "db"),
            P(None, "db"),
            P("db", None),
            P("seq", None, None),
            P(),
            P(),
        ),
        out_specs=P(("seq", "db"), None),
        check_vma=False,
    )
```

```python
import functools
import math

import jax
import jax.numpy as jnp
from jax import lax
from jax.experimental import pallas as pl
from jax.experimental.pallas import tpu as pltpu
from jax.sharding import PartitionSpec as P

HS = 128
CL = 64
NB_LEN = 128
NEIGH = 2


def shifted(value, axis, steps):
    count = lax.axis_size(axis)
    first, last = (max(0, -steps), min(count, count - steps))
    return lax.ppermute(value, axis, [(source, source + steps) for source in range(first, last)])


def bucket_places(shards):
    count = shards.shape[1]
    same_shard = shards[:, :, None] == shards[:, None, :]
    earlier = jnp.arange(count)[None, :] < jnp.arange(count)[:, None]
    return jnp.sum((same_shard & earlier[None]).astype(jnp.int32), axis=2)


def attend_kernel(first, entries, *refs):
    per_step = (len(refs) - 3) // 3
    q_refs, row_refs = refs[:per_step], refs[per_step : 3 * per_step]
    wk_ref, wv_ref, o_ref = refs[3 * per_step :]
    rows = jnp.concatenate([ref[0] for ref in row_refs], axis=0)
    keys = jnp.dot(rows, wk_ref[...], preferred_element_type=jnp.float32).astype(jnp.bfloat16)
    keys_len, qlen = keys.shape[0] // per_step, q_refs[0].shape[1]
    pair = 2 * HS if keys.shape[1] % (2 * HS) == 0 else HS
    units = [
        (place, slice(place * keys_len, (place + 1) * keys_len), at)
        for place in range(per_step)
        for at in range(0, keys.shape[1], pair)
    ]
    blank = jnp.zeros((qlen, HS), jnp.bfloat16)

    def spread(place, at):
        if pair == HS:
            return q_refs[place][0, :, at : at + HS]
        low = jnp.concatenate([q_refs[place][0, :, at : at + HS], blank], axis=1)
        high = jnp.concatenate([blank, q_refs[place][0, :, at + HS : at + pair]], axis=1)
        return jnp.concatenate([low, high], axis=0)

    scores = jnp.concatenate(
        [
            lax.dot_general(
                spread(place, at),
                keys[here, at : at + pair],
                (((1,), (1,)), ((), ())),
                preferred_element_type=jnp.float32,
            )
            for place, here, at in units
        ],
        axis=0,
    )
    values = jnp.dot(rows, wv_ref[...], preferred_element_type=jnp.float32).astype(jnp.bfloat16)
    top = jnp.max(scores, axis=-1, keepdims=True)
    weights = jnp.exp((scores - top) * (1.0 / math.sqrt(HS)))
    probs = weights * (1.0 / jnp.sum(weights, axis=-1, keepdims=True))
    probs = probs.astype(jnp.bfloat16)
    size = qlen * (pair // HS)
    for unit, (place, here, at) in enumerate(units):
        mixed = jnp.dot(
            probs[unit * size : (unit + 1) * size],
            values[here, at : at + pair],
            preferred_element_type=jnp.float32,
        ).astype(jnp.bfloat16)
        for part in range(pair // HS):
            o_ref[place, :, at + part * HS : at + (part + 1) * HS] = mixed[
                part * qlen : (part + 1) * qlen, part * HS : (part + 1) * HS
            ]


def attend(first, count, entries, queries, rows, w_key, w_value):
    per_step = 2 if count % 2 == 0 else 1
    _, qlen, width = queries.shape
    _, nb_len, depth = rows.shape

    def query_block(place):
        return pl.BlockSpec(
            (1, qlen, width), lambda g, f, e: (f[0] + g * per_step + place, 0, 0)
        )

    def row_block(place, which):
        return pl.BlockSpec(
            (1, nb_len, depth),
            lambda g, f, e: (e[(f[0] + g * per_step + place) * NEIGH + which], 0, 0),
        )

    whole = pl.BlockSpec((depth, width), lambda g, f, e: (0, 0))
    grid_spec = pltpu.PrefetchScalarGridSpec(
        num_scalar_prefetch=2,
        grid=(count // per_step,),
        in_specs=[query_block(place) for place in range(per_step)]
        + [row_block(place, which) for place in range(per_step) for which in range(NEIGH)]
        + [whole, whole],
        out_specs=pl.BlockSpec((per_step, qlen, width), lambda g, f, e: (g, 0, 0)),
    )
    operands = [queries] * per_step + [rows] * (NEIGH * per_step) + [w_key, w_value]
    return pl.pallas_call(
        attend_kernel,
        grid_spec=grid_spec,
        out_shape=jax.ShapeDtypeStruct((count, qlen, width), jnp.bfloat16),
        compiler_params=pltpu.CompilerParams(vmem_limit_bytes=56 * 1024 * 1024),
        cost_estimate=pl.CostEstimate(flops=1000, bytes_accessed=1000, transcendentals=0),
        name="attend",
    )(first.reshape(1).astype(jnp.int32), entries, *operands)


def project_kernel(x_ref, y_ref, z_ref, wx_ref, wy_ref, wz_ref, rest_ref, last_ref):
    total = jnp.dot(x_ref[...], wx_ref[...], preferred_element_type=jnp.float32)
    total += jnp.dot(y_ref[...], wy_ref[...], preferred_element_type=jnp.float32)
    total += jnp.dot(z_ref[...], wz_ref[...], preferred_element_type=jnp.float32)
    total = total.astype(jnp.bfloat16)
    cut = rest_ref.shape[0]
    rest_ref[...] = total[:cut]
    last_ref[...] = total[cut:]


def project(x, y, z, w_x, w_y, w_z):
    size, width = x.shape
    features = w_x.shape[1]
    tile = 512
    own = lambda array: pl.BlockSpec(array.shape, lambda g: (0, 0))
    strip = lambda array: pl.BlockSpec((array.shape[0], tile), lambda g: (0, g))
    return pl.pallas_call(
        project_kernel,
        grid=(features // tile,),
        in_specs=[own(x), own(y), own(z), strip(w_x), strip(w_y), strip(w_z)],
        out_specs=[
            pl.BlockSpec((size // 2, tile), lambda g: (0, g)),
            pl.BlockSpec((size // 2, tile), lambda g: (0, g)),
        ],
        out_shape=[
            jax.ShapeDtypeStruct((size // 2, features), jnp.bfloat16),
            jax.ShapeDtypeStruct((size // 2, features), jnp.bfloat16),
        ],
        compiler_params=pltpu.CompilerParams(vmem_limit_bytes=40 * 1024 * 1024),
        cost_estimate=pl.CostEstimate(flops=1000, bytes_accessed=1000, transcendentals=0),
        name="project",
    )(x, y, z, w_x, w_y, w_z)


def body(decoder, w_query, w_key, w_value, w_out, database, nb_shard, nb_slot):
    n_seq = lax.axis_size("seq")
    n_db = lax.axis_size("db")
    seq_index = lax.axis_index("seq")
    db_index = lax.axis_index("db")
    tok_rows = decoder.shape[0]
    spans_dev = tok_rows // CL
    width = w_query.shape[1]
    requests = NEIGH * spans_dev
    capacity = (requests + n_seq - 1) // n_seq + 1
    shard_lists = nb_shard.reshape(n_seq, requests)
    slot_lists = nb_slot.reshape(n_seq, requests)
    places = bucket_places(shard_lists)
    mine = shard_lists == seq_index
    picked = mine[:, None, :] & (places[:, None, :] == jnp.arange(capacity)[None, :, None])
    send_slot = jnp.sum(jnp.where(picked, slot_lists[:, None, :], 0), axis=2)
    outgoing = database[send_slot]
    received = lax.all_to_all(outgoing, "seq", split_axis=0, concat_axis=0, tiled=True)
    my_shards = lax.dynamic_index_in_dim(shard_lists, seq_index, 0, keepdims=False)
    my_places = lax.dynamic_index_in_dim(places, seq_index, 0, keepdims=False)
    entries = my_shards * capacity + my_places
    rows = received.reshape(n_seq * capacity, NB_LEN, received.shape[3])
    swap = [(source, source ^ 1) for source in range(n_db)]
    half = w_out.shape[0] // 2
    my_half = lax.rem(seq_index, 2)
    w_near = lax.ppermute(
        lax.dynamic_slice_in_dim(w_out, my_half * half, half, 0), "db", swap
    )
    source = decoder.astype(jnp.float32)
    scale = lax.rsqrt(jnp.mean(source * source, axis=-1, keepdims=True) + 1e-05)
    normed = (source * scale).astype(jnp.bfloat16)
    queries = jnp.dot(normed, w_query, preferred_element_type=jnp.float32).astype(jnp.bfloat16)
    incoming = shifted(queries[: CL - 1], "seq", -1)
    aligned_queries = jnp.concatenate([queries[CL - 1 :], incoming], axis=0).reshape(
        spans_dev, CL, width
    )
    w_near, rows, aligned_queries = lax.optimization_barrier((w_near, rows, aligned_queries))
    near_seq = [(source, source ^ 1) for source in range(n_seq)]
    w_far = lax.ppermute(w_near, "seq", near_seq)
    blocks = n_db // 2
    block_spans = spans_dev // n_db

    def attend_block(owner, step, queries):
        first = lax.rem(owner + 2 * step, n_db) * block_spans
        return attend(first, block_spans, entries, queries, rows, w_key, w_value)

    def partial_of(step, queries):
        theirs = attend_block(db_index ^ 1, step, queries)
        from_pair = lax.ppermute(theirs, "db", swap).reshape(-1, width)
        ours = attend_block(db_index, step, queries)
        near = lax.dynamic_slice_in_dim(from_pair, my_half * half, half, 1)
        far = lax.dynamic_slice_in_dim(from_pair, (1 - my_half) * half, half, 1)
        return project(ours.reshape(-1, width), near, far, w_out, w_near, w_far)

    rests, lasts = [], []
    for step in range(1, blocks):
        rest, last = partial_of(step, aligned_queries)
        pairs = [(source, (source + 2 * step) % n_db) for source in range(n_db)]
        lasts.append(lax.ppermute(last, "db", pairs))
        rests.append(lax.ppermute(rest, "db", pairs))
    rest, last = partial_of(0, aligned_queries)
    last = sum([value.astype(jnp.float32) for value in lasts], last.astype(jnp.float32))
    last = last.astype(jnp.bfloat16)
    flat = n_seq * n_db
    halo = lax.ppermute(
        last[-(CL - 1) :], ("seq", "db"), [(source, source + 1) for source in range(flat - 1)]
    )
    rest = sum([value.astype(jnp.float32) for value in rests], rest.astype(jnp.float32))
    return jnp.concatenate([halo, rest.astype(jnp.bfloat16), last[: -(CL - 1)]], axis=0)


def solution(mesh):
    return jax.shard_map(
        body,
        mesh=mesh,
        in_specs=(
            P("seq", None),
            P(None, "db"),
            P(None, "db"),
            P(None, "db"),
            P("db", None),
            P("seq", None, None),
            P(),
            P(),
        ),
        out_specs=P(("seq", "db"), None),
        check_vma=False,
    )
```

```python
import functools
import math

import jax
import jax.numpy as jnp
from jax import lax
from jax.experimental import pallas as pl
from jax.experimental.pallas import tpu as pltpu
from jax.sharding import PartitionSpec as P

HS = 128
CL = 64
NB_LEN = 128
NEIGH = 2


def shifted(value, axis, steps):
    count = lax.axis_size(axis)
    first, last = (max(0, -steps), min(count, count - steps))
    return lax.ppermute(value, axis, [(source, source + steps) for source in range(first, last)])


def bucket_places(shards):
    count = shards.shape[1]
    same_shard = shards[:, :, None] == shards[:, None, :]
    earlier = jnp.arange(count)[None, :] < jnp.arange(count)[:, None]
    return jnp.sum((same_shard & earlier[None]).astype(jnp.int32), axis=2)


def attend_kernel(first, entries, *refs):
    per_step = (len(refs) - 3) // 3
    q_refs, row_refs = refs[:per_step], refs[per_step : 3 * per_step]
    wk_ref, wv_ref, o_ref = refs[3 * per_step :]
    rows = jnp.concatenate([ref[0] for ref in row_refs], axis=0)
    keys = jnp.dot(rows, wk_ref[...], preferred_element_type=jnp.float32).astype(jnp.bfloat16)
    keys_len, qlen = keys.shape[0] // per_step, q_refs[0].shape[1]
    pair = 2 * HS if keys.shape[1] % (2 * HS) == 0 else HS
    units = [
        (place, slice(place * keys_len, (place + 1) * keys_len), at)
        for place in range(per_step)
        for at in range(0, keys.shape[1], pair)
    ]
    blank = jnp.zeros((qlen, HS), jnp.bfloat16)

    def spread(place, at):
        if pair == HS:
            return q_refs[place][0, :, at : at + HS]
        low = jnp.concatenate([q_refs[place][0, :, at : at + HS], blank], axis=1)
        high = jnp.concatenate([blank, q_refs[place][0, :, at + HS : at + pair]], axis=1)
        return jnp.concatenate([low, high], axis=0)

    scores = jnp.concatenate(
        [
            lax.dot_general(
                spread(place, at),
                keys[here, at : at + pair],
                (((1,), (1,)), ((), ())),
                preferred_element_type=jnp.float32,
            )
            for place, here, at in units
        ],
        axis=0,
    )
    values = jnp.dot(rows, wv_ref[...], preferred_element_type=jnp.float32).astype(jnp.bfloat16)
    top = jnp.max(scores, axis=-1, keepdims=True)
    weights = jnp.exp((scores - top) * (1.0 / math.sqrt(HS)))
    probs = weights * (1.0 / jnp.sum(weights, axis=-1, keepdims=True))
    probs = probs.astype(jnp.bfloat16)
    size = qlen * (pair // HS)
    for unit, (place, here, at) in enumerate(units):
        mixed = jnp.dot(
            probs[unit * size : (unit + 1) * size],
            values[here, at : at + pair],
            preferred_element_type=jnp.float32,
        ).astype(jnp.bfloat16)
        for part in range(pair // HS):
            o_ref[place, :, at + part * HS : at + (part + 1) * HS] = mixed[
                part * qlen : (part + 1) * qlen, part * HS : (part + 1) * HS
            ]


def attend(first, count, entries, queries, rows, w_key, w_value):
    per_step = 2 if count % 2 == 0 else 1
    _, qlen, width = queries.shape
    _, nb_len, depth = rows.shape

    def query_block(place):
        return pl.BlockSpec(
            (1, qlen, width), lambda g, f, e: (f[0] + g * per_step + place, 0, 0)
        )

    def row_block(place, which):
        return pl.BlockSpec(
            (1, nb_len, depth),
            lambda g, f, e: (e[(f[0] + g * per_step + place) * NEIGH + which], 0, 0),
        )

    whole = pl.BlockSpec((depth, width), lambda g, f, e: (0, 0))
    grid_spec = pltpu.PrefetchScalarGridSpec(
        num_scalar_prefetch=2,
        grid=(count // per_step,),
        in_specs=[query_block(place) for place in range(per_step)]
        + [row_block(place, which) for place in range(per_step) for which in range(NEIGH)]
        + [whole, whole],
        out_specs=pl.BlockSpec((per_step, qlen, width), lambda g, f, e: (g, 0, 0)),
    )
    operands = [queries] * per_step + [rows] * (NEIGH * per_step) + [w_key, w_value]
    return pl.pallas_call(
        attend_kernel,
        grid_spec=grid_spec,
        out_shape=jax.ShapeDtypeStruct((count, qlen, width), jnp.bfloat16),
        compiler_params=pltpu.CompilerParams(vmem_limit_bytes=56 * 1024 * 1024),
        cost_estimate=pl.CostEstimate(flops=1000, bytes_accessed=1000, transcendentals=0),
        name="attend",
    )(first.reshape(1).astype(jnp.int32), entries, *operands)


def project_kernel(x_ref, y_ref, z_ref, wx_ref, wy_ref, wz_ref, *out_refs):
    total = jnp.dot(x_ref[...], wx_ref[...], preferred_element_type=jnp.float32)
    total += jnp.dot(y_ref[...], wy_ref[...], preferred_element_type=jnp.float32)
    total += jnp.dot(z_ref[...], wz_ref[...], preferred_element_type=jnp.float32)
    total = total.astype(jnp.bfloat16)
    size = out_refs[0].shape[0]
    for at, ref in enumerate(out_refs):
        ref[...] = total[at * size : (at + 1) * size]


def project(parts, x, y, z, w_x, w_y, w_z):
    size = x.shape[0] // parts
    features = w_x.shape[1]
    tile = 512
    own = lambda array: pl.BlockSpec(array.shape, lambda g: (0, 0))
    strip = lambda array: pl.BlockSpec((array.shape[0], tile), lambda g: (0, g))
    return pl.pallas_call(
        project_kernel,
        grid=(features // tile,),
        in_specs=[own(x), own(y), own(z), strip(w_x), strip(w_y), strip(w_z)],
        out_specs=[pl.BlockSpec((size, tile), lambda g: (0, g))] * parts,
        out_shape=[jax.ShapeDtypeStruct((size, features), jnp.bfloat16)] * parts,
        compiler_params=pltpu.CompilerParams(vmem_limit_bytes=40 * 1024 * 1024),
        cost_estimate=pl.CostEstimate(flops=1000, bytes_accessed=1000, transcendentals=0),
        name="project",
    )(x, y, z, w_x, w_y, w_z)


def body(decoder, w_query, w_key, w_value, w_out, database, nb_shard, nb_slot):
    n_seq = lax.axis_size("seq")
    n_db = lax.axis_size("db")
    seq_index = lax.axis_index("seq")
    db_index = lax.axis_index("db")
    tok_rows = decoder.shape[0]
    spans_dev = tok_rows // CL
    width = w_query.shape[1]
    requests = NEIGH * spans_dev
    capacity = (requests + n_seq - 1) // n_seq + 1
    shard_lists = nb_shard.reshape(n_seq, requests)
    slot_lists = nb_slot.reshape(n_seq, requests)
    places = bucket_places(shard_lists)
    mine = shard_lists == seq_index
    picked = mine[:, None, :] & (places[:, None, :] == jnp.arange(capacity)[None, :, None])
    send_slot = jnp.sum(jnp.where(picked, slot_lists[:, None, :], 0), axis=2)
    outgoing = database[send_slot]
    received = lax.all_to_all(outgoing, "seq", split_axis=0, concat_axis=0, tiled=True)
    my_shards = lax.dynamic_index_in_dim(shard_lists, seq_index, 0, keepdims=False)
    my_places = lax.dynamic_index_in_dim(places, seq_index, 0, keepdims=False)
    entries = my_shards * capacity + my_places
    rows = received.reshape(n_seq * capacity, NB_LEN, received.shape[3])
    swap = [(source, source ^ 1) for source in range(n_db)]
    half = w_out.shape[0] // 2
    my_half = lax.rem(seq_index, 2)
    w_near = lax.ppermute(
        lax.dynamic_slice_in_dim(w_out, my_half * half, half, 0), "db", swap
    )
    source = decoder.astype(jnp.float32)
    scale = lax.rsqrt(jnp.mean(source * source, axis=-1, keepdims=True) + 1e-05)
    normed = (source * scale).astype(jnp.bfloat16)
    queries = jnp.dot(normed, w_query, preferred_element_type=jnp.float32).astype(jnp.bfloat16)
    incoming = shifted(queries[: CL - 1], "seq", -1)
    aligned_queries = jnp.concatenate([queries[CL - 1 :], incoming], axis=0).reshape(
        spans_dev, CL, width
    )
    w_near, rows, aligned_queries = lax.optimization_barrier((w_near, rows, aligned_queries))
    near_seq = [(source, source ^ 1) for source in range(n_seq)]
    w_far = lax.ppermute(w_near, "seq", near_seq)
    blocks = n_db // 2
    block_spans = spans_dev // n_db

    half_spans = block_spans // 2

    def context_of(owner, step, inner, count, queries):
        first = lax.rem(owner + 2 * step, n_db) * block_spans + inner
        return attend(first, count, entries, queries, rows, w_key, w_value)

    from_pair = {}
    for step in [*range(1, blocks), 0]:
        theirs = context_of(db_index ^ 1, step, 0, block_spans, aligned_queries)
        theirs, aligned_queries = lax.optimization_barrier((theirs, aligned_queries))
        from_pair[step] = lax.ppermute(theirs, "db", swap)

    def partial_of(step, inner, count, queries):
        ours = context_of(db_index, step, inner, count, queries).reshape(-1, width)
        other = from_pair[step][inner : inner + count].reshape(-1, width)
        near = lax.dynamic_slice_in_dim(other, my_half * half, half, 1)
        far = lax.dynamic_slice_in_dim(other, (1 - my_half) * half, half, 1)
        return project(count // half_spans, ours, near, far, w_out, w_near, w_far)

    rests, lasts = [], []
    for step in range(1, blocks):
        pairs = [(source, (source + 2 * step) % n_db) for source in range(n_db)]
        for inner, sums in ((half_spans, lasts), (0, rests)):
            (partial,) = partial_of(step, inner, half_spans, aligned_queries)
            partial, aligned_queries, from_pair[0] = lax.optimization_barrier(
                (partial, aligned_queries, from_pair[0])
            )
            sums.append(lax.ppermute(partial, "db", pairs))
    rest, last = partial_of(0, 0, block_spans, aligned_queries)
    last = sum([value.astype(jnp.float32) for value in lasts], last.astype(jnp.float32))
    last = last.astype(jnp.bfloat16)
    flat = n_seq * n_db
    halo = lax.ppermute(
        last[-(CL - 1) :], ("seq", "db"), [(source, source + 1) for source in range(flat - 1)]
    )
    rest = sum([value.astype(jnp.float32) for value in rests], rest.astype(jnp.float32))
    return jnp.concatenate([halo, rest.astype(jnp.bfloat16), last[: -(CL - 1)]], axis=0)


def solution(mesh):
    return jax.shard_map(
        body,
        mesh=mesh,
        in_specs=(
            P("seq", None),
            P(None, "db"),
            P(None, "db"),
            P(None, "db"),
            P("db", None),
            P("seq", None, None),
            P(),
            P(),
        ),
        out_specs=P(("seq", "db"), None),
        check_vma=False,
    )
```
